128 devices in a mesh: frame: 8 (over x_hi, z), patch: 16 (over y, x_lo, core).
Axes of the slice: x: 4 (x_hi: 2, x_lo: 2; x = x_hi * 2 + x_lo), y: 4, z: 4, core: 2. Of those that a mesh axis runs over, the one named last changes fastest.
Arguments:
- latent: bfloat16 [32768, 1536], P(('frame', 'patch')), parts along dimension 0, may hold values from -6 to 6
- conv_weight: float32 [9, 1536], replicated, may hold values from -4 to 4
- time_table: bfloat16 [50, 4608], replicated
- action_table: bfloat16 [18, 4608], replicated
- timestep: int32 [8], P('frame'), parts along dimension 0, may hold values from 0 to 49
- action: int32 [8], P('frame'), parts along dimension 0, may hold values from 0 to 17
- w_qkv: bfloat16 [1536, 4608], replicated, may hold values from -0.21875 to 0.21875
- w_out: bfloat16 [1536, 1536], replicated, may hold values from -0.15625 to 0.15625
- stale_kv: bfloat16 [32768, 3072], P(('frame', 'patch')), parts along dimension 0
Outputs:
- layer_out: bfloat16 [32768, 1536], P(('frame', 'patch')), parts along dimension 0
- fresh_kv: bfloat16 [32768, 3072], P(('frame', 'patch')), parts along dimension 0
The draws below stay inside these ranges and needn't reach their ends.
There are 8 independent parts, one for each index of `frame`. The reference program is written for one: setup_inputs(seed, part) draws one part's arguments, and reference() takes and returns one part's arrays. A program takes and returns all parts, laid end to end along the dimension named above; an argument that names none is the same for every part. Nothing has to cross between parts.
All inputs are finite; a program needn't handle non-finite values.
Results may differ from the reference program's by a relative error of at most 0.012.
Values may be sent and summed in bfloat16 or wider, within the bound.
No kernel may reach another device: no remote copies, remote signals or barrier semaphores. Data moves between devices by JAX's collectives and lax.ppermute only.
A program may use at most 128 MiB of HBM per device.

```python
import jax
import jax.numpy as jnp
from jax import lax

HEADS = 24
HD = 64
D = 1536
GRID_W = 64
STEPS = 50
ACTIONS = 18
TOK_DEV = 256
TOKENS = 4096
N_PATCH = 16


def module_rows(key, count):
    base = jnp.clip(jax.random.normal(key, (count, 3 * D), jnp.float32), -6.0, 6.0)
    column = jnp.arange(3 * D, dtype=jnp.int32)[None, :]
    factor = jnp.where(column < D, 0.15, jnp.where(column < 2 * D, 0.25, 0.6))
    return (base * factor).astype(jnp.bfloat16)


def draw_time_table(key, part):
    key = jax.random.fold_in(key, 11)
    return module_rows(key, STEPS)


def draw_action_table(key, part):
    key = jax.random.fold_in(key, 13)
    return module_rows(key, ACTIONS)


def draw_stale_kv(key, part):
    key = jax.random.fold_in(key, 7)
    first = jax.random.fold_in(key, 0)
    column = jnp.arange(2 * D, dtype=jnp.int32)[None, :]
    base = jnp.clip(jax.random.normal(first, (TOKENS, 2 * D), jnp.float32), -5.0, 5.0)
    base = base * jnp.where(column < D, 1.5, 2.2)
    return base.astype(jnp.bfloat16)


def level_of(own_key, extent, shards, low, high):
    gain = 1.0
    for position, parts in shards:
        heights = jax.random.uniform(jax.random.fold_in(jax.random.fold_in(own_key, 6), position), (parts,), jnp.float32, low / len(shards), high / len(shards))
        gain = gain * jnp.repeat(jnp.exp(heights), extent[position] // parts).reshape((-1,) + (1,) * (len(extent) - 1 - position))
    return gain


def bell_draw(rng, dims, spread, limit, pieces=(), kind=jnp.bfloat16):
    values = jax.random.normal(rng, dims, jnp.float32) * spread
    if len(pieces) > 0:
        values = level_of(rng, dims, pieces, -0.22, 0.18) * values
    return jnp.clip(values, min=-limit, max=limit).astype(kind)


def setup_inputs(seed: int = 0, part: int = 0) -> dict:
    seeds = jax.random.split(jax.random.key(seed), 10)
    part_splits = jax.random.split(jax.random.fold_in(seeds[9], part), 10)
    latent = bell_draw(part_splits[0], (TOKENS, D), 1.0, 6.0, ((0, 16),))
    conv_weight = bell_draw(seeds[1], (9, D), 0.3, 4.0, (), jnp.float32)
    time_table = draw_time_table(jax.random.fold_in(seeds[9], 71), part)
    action_table = draw_action_table(jax.random.fold_in(seeds[9], 71), part)
    timestep = jax.random.randint(part_splits[4], (1,), 0, STEPS).astype(jnp.int32)
    action = jax.random.randint(part_splits[5], (1,), 0, ACTIONS).astype(jnp.int32)
    w_qkv = bell_draw(seeds[6], (D, 3 * D), (D // 2) ** -0.5, 0.21875)
    w_out = bell_draw(seeds[7], (D, D), D ** -0.5, 0.15625)
    stale_kv = draw_stale_kv(jax.random.fold_in(jax.random.fold_in(seeds[9], part), 71), part)
    return dict(latent=latent, conv_weight=conv_weight, time_table=time_table, action_table=action_table, timestep=timestep, action=action, w_qkv=w_qkv, w_out=w_out, stale_kv=stale_kv)


def lookup(table, index):
    hot = (jnp.arange(table.shape[0], dtype=jnp.int32)[None, :] == index[:, None]).astype(table.dtype)
    return jnp.dot(hot, table, preferred_element_type=jnp.float32)[0]

def reference(latent, conv_weight, time_table, action_table, timestep, action, w_qkv, w_out, stale_kv):
    grid = latent.astype(jnp.float32).reshape(-1, GRID_W, D)
    nrows = grid.shape[0]
    padded = jnp.pad(grid, ((1, 1), (1, 1), (0, 0)))
    mixed = grid
    for a in range(3):
        for b in range(3):
            mixed = mixed + padded[a:a + nrows, b:b + GRID_W] * conv_weight[3 * a + b]
    mixed = mixed.reshape(-1, D)
    modulation = lookup(time_table, timestep) + lookup(action_table, action)
    shift, scale, gate = (modulation[:D], modulation[D:2 * D], modulation[2 * D:])
    mean = lax.optimization_barrier(jnp.mean(mixed, axis=1, keepdims=True))
    var = lax.optimization_barrier(jnp.mean((mixed - mean) ** 2, axis=1, keepdims=True))
    normed = ((mixed - mean) * lax.rsqrt(var + 1e-06) * (1.0 + scale) + shift).astype(jnp.bfloat16)
    projected = jnp.dot(normed, w_qkv, preferred_element_type=jnp.float32)
    queries = projected[:, :D].astype(jnp.bfloat16)
    fresh_kv = projected[:, D:].astype(jnp.bfloat16)

    def block_out(blk):
        first = (blk * TOK_DEV).astype(jnp.int32)
        query = lax.dynamic_slice_in_dim(queries, first, TOK_DEV, 0).reshape(TOK_DEV, HEADS, HD).astype(jnp.float32)
        own = lax.dynamic_slice_in_dim(fresh_kv, first, TOK_DEV, 0)
        whole = lax.dynamic_update_slice_in_dim(stale_kv, own, first, 0)
        keys = whole[:, :D].reshape(-1, HEADS, HD).astype(jnp.float32)
        values = whole[:, D:].reshape(-1, HEADS, HD).astype(jnp.float32)
        scores = jnp.einsum('qhe,khe->hqk', query, keys) * HD ** (-0.5)
        top = lax.optimization_barrier(jnp.max(scores, axis=2, keepdims=True))
        expo = jnp.exp(scores - top)
        total = lax.optimization_barrier(jnp.sum(expo, axis=2))
        weights = lax.optimization_barrier(expo.astype(jnp.bfloat16))
        summed = jnp.einsum('hqk,khe->hqe', weights.astype(jnp.float32), values)
        result = summed / total[:, :, None]
        return jnp.transpose(result, (1, 0, 2)).reshape(TOK_DEV, D).astype(jnp.bfloat16)
    attended = lax.map(block_out, jnp.arange(N_PATCH, dtype=jnp.int32)).reshape(-1, D)
    proj = jnp.dot(attended, w_out, preferred_element_type=jnp.float32)
    layer_out = (mixed + gate * proj).astype(jnp.bfloat16)
    return (layer_out, fresh_kv)
```

```python
import functools
import math

import jax
import jax.numpy as jnp
from jax import lax
from jax.experimental import pallas as pl
from jax.experimental.pallas import tpu as pltpu
from jax.sharding import PartitionSpec as P

HEADS = 24
HD = 64
GRID_W = 64
ROWS = 256
D = 1536
CHIPS = 8
GROUP = 3 * HD
STATS = 16
KV_ROWS = 768
QSCALE = 1.0 / math.sqrt(HD)
F32 = jnp.float32
BF16 = jnp.bfloat16
VMEM = pl.BlockSpec(memory_space=pltpu.VMEM)
ANY = pl.BlockSpec(memory_space=pl.ANY)


def mm(a, b):
    return lax.dot_general(a, b, (((1,), (0,)), ((), ())), preferred_element_type=F32)


KEY_ROWS = 384


def pack_kernel(kv_hbm, out_hbm, kv, out, sems):
    reads = []
    for n, (first, count) in enumerate(((0, D), (D, 1024), (D + 1024, 512))):
        cols = pl.ds(first, count)
        reads.append(pltpu.make_async_copy(kv_hbm.at[:, cols], kv.at[:, cols], sems.at[n]))
    for copy in reads:
        copy.start()

    def write(first, count, n):
        rows = pl.ds(first, count)
        copy = pltpu.make_async_copy(out.at[:, rows], out_hbm.at[:, rows], sems.at[n])
        copy.start()
        return copy

    reads[0].wait()
    for j in range(CHIPS):
        out[j, 0:256, :] = kv[:, 128 * j : 128 * (j + 1)]
        col = 1024 + 64 * j
        out[j, 256:KEY_ROWS, :] = jnp.concatenate(
            [kv[0:128, col : col + 64], kv[128:256, col : col + 64]], axis=1
        )
    keys = write(0, KEY_ROWS, 3)
    for t in range(12):
        if t % 8 == 0:
            reads[1 + t // 8].wait()
        vt = kv[:, D + 128 * t : D + 128 * (t + 1)].T
        if t < 8:
            out[t, 384:512, :] = vt[:, 0:128]
            out[t, 576:704, :] = vt[:, 128:256]
        else:
            for half in range(2):
                j = 2 * (t - 8) + half
                part = vt[64 * half : 64 * half + 64]
                out[j, 512:576, :] = part[:, 0:128]
                out[j, 704:768, :] = part[:, 128:256]
    values = write(KEY_ROWS, KV_ROWS - KEY_ROWS, 4)
    keys.wait()
    values.wait()


def pack(stale_kv):
    return pl.pallas_call(
        pack_kernel,
        out_shape=jax.ShapeDtypeStruct((CHIPS, KV_ROWS, 128), BF16),
        in_specs=[ANY],
        out_specs=ANY,
        scratch_shapes=[
            pltpu.VMEM((ROWS, 2 * D), BF16),
            pltpu.VMEM((CHIPS, KV_ROWS, 128), BF16),
            pltpu.SemaphoreType.DMA((5,)),
        ],
        compiler_params=pltpu.CompilerParams(vmem_limit_bytes=54 * 2**20),
        name="pack_kv",
    )(stale_kv)


W_COLS = 512
W_BLOCKS = 3 * D // W_COLS


def qkv_kernel(
    patch_ref,
    step_ref,
    act_ref,
    lat_ref,
    inner_ref,
    outer_ref,
    cw_ref,
    time_ref,
    action_ref,
    w_hbm,
    q_ref,
    kv_ref,
    mixed_ref,
    gate_ref,
    w_buf,
    ext,
    normed,
    sems,
):
    for c in range(W_BLOCKS):
        pltpu.make_async_copy(
            w_hbm.at[:, pl.ds(c * W_COLS, W_COLS)], w_buf.at[c], sems.at[c]
        ).start()
    patch = patch_ref[0]
    first_core = lax.rem(patch, 2) == 0
    inner, outer = inner_ref[...].astype(F32), outer_ref[...].astype(F32)
    ext[0:64, :] = jnp.where(first_core, outer, inner)
    ext[64:320, :] = lat_ref[...].astype(F32)
    ext[320:384, :] = jnp.where(first_core, inner, outer)

    def lookup(table, index):
        count = table.shape[0]
        hot = (lax.broadcasted_iota(jnp.int32, (16, count), 1) == index).astype(BF16)
        return mm(hot, table[...])[0:1, :]

    modulation = lookup(time_ref, step_ref[0]) + lookup(action_ref, act_ref[0])
    gate_ref[...] = modulation[:, 2 * D :]
    place = lax.rem(lax.broadcasted_iota(jnp.int32, (ROWS, 128), 0), GRID_W)
    not_first = place != 0
    not_last = place != GRID_W - 1
    total = jnp.zeros((ROWS, 128), F32)
    for t in range(D // 128):
        cols = slice(128 * t, 128 * (t + 1))
        a = [ext[64 * k : 64 * k + 256, cols] for k in range(3)]
        w = [cw_ref[k : k + 1, cols] for k in range(9)]
        left = a[0] * w[0] + a[1] * w[3] + a[2] * w[6]
        mid = a[0] * w[1] + a[1] * w[4] + a[2] * w[7]
        right = a[0] * w[2] + a[1] * w[5] + a[2] * w[8]
        left = jnp.where(not_first, pltpu.roll(left, 1, 0), 0.0)
        right = jnp.where(not_last, pltpu.roll(right, ROWS - 1, 0), 0.0)
        m = a[1] + mid + left + right
        mixed_ref[:, cols] = m
        total = total + m
    mean = jnp.sum(total, axis=1, keepdims=True) * (1.0 / D)
    square = jnp.zeros((ROWS, 128), F32)
    for t in range(D // 128):
        m = mixed_ref[:, 128 * t : 128 * (t + 1)] - mean
        square = square + m * m
    inv = lax.rsqrt(jnp.sum(square, axis=1, keepdims=True) * (1.0 / D) + 1e-06)
    for t in range(D // 128):
        cols = slice(128 * t, 128 * (t + 1))
        shift = modulation[:, 128 * t : 128 * (t + 1)]
        scale = modulation[:, D + 128 * t : D + 128 * (t + 1)]
        normed[:, cols] = (
            (mixed_ref[:, cols] - mean) * inv * (1.0 + scale) + shift
        ).astype(BF16)
    for c in range(W_BLOCKS):
        pltpu.make_async_copy(
            w_hbm.at[:, pl.ds(c * W_COLS, W_COLS)], w_buf.at[c], sems.at[c]
        ).wait()
        out = mm(normed[...], w_buf[c])
        if c < D // W_COLS:
            qt = (out * QSCALE).astype(BF16).T
            for t in range(W_COLS // 128):
                tile = c * (W_COLS // 128) + t
                if tile < 8:
                    q_ref[tile, 0:128, :] = qt[128 * t : 128 * t + 128]
                else:
                    for half in range(2):
                        first = 128 * t + 64 * half
                        q_ref[2 * (tile - 8) + half, 128:192, :] = qt[first : first + 64]
        else:
            col = c * W_COLS - D
            kv_ref[:, col : col + W_COLS] = out.astype(BF16)


def qkv(patch, timestep, action, latent, inner, outer, conv_weight, time_table, action_table, w_qkv):
    smem = pl.BlockSpec(memory_space=pltpu.SMEM)
    return pl.pallas_call(
        qkv_kernel,
        out_shape=(
            jax.ShapeDtypeStruct((CHIPS, GROUP, ROWS), BF16),
            jax.ShapeDtypeStruct((ROWS, 2 * D), BF16),
            jax.ShapeDtypeStruct((ROWS, D), F32),
            jax.ShapeDtypeStruct((1, D), F32),
        ),
        in_specs=[smem] * 3 + [VMEM] * 6 + [ANY],
        out_specs=(VMEM,) * 4,
        scratch_shapes=[
            pltpu.VMEM((W_BLOCKS, D, W_COLS), BF16),
            pltpu.VMEM((ROWS + 2 * GRID_W, D), F32),
            pltpu.VMEM((ROWS, D), BF16),
            pltpu.SemaphoreType.DMA((W_BLOCKS,)),
        ],
        compiler_params=pltpu.CompilerParams(vmem_limit_bytes=40 * 2**20),
        cost_estimate=pl.CostEstimate(
            flops=40 * 2 * ROWS * D * 3 * D, bytes_accessed=20 * 2**20, transcendentals=0
        ),
        name="conv_norm_qkv",
    )(patch, timestep, action, latent, inner, outer, conv_weight, time_table, action_table, w_qkv)


def own_kernel(q_ref, kv_ref, tie_ref, o_ref, lse_ref, s_a, s_b):
    del tie_ref
    zeros = jnp.zeros((HD, ROWS), BF16)
    ones = jnp.ones((STATS, ROWS), BF16)
    buffers = (s_a, s_b)

    def scores(tile):
        buf = buffers[tile % 2]
        keys = kv_ref[:, 128 * tile : 128 * tile + 128]
        tops = []
        for half in range(2):
            if tile < 8:
                q = q_ref[tile, 64 * half : 64 * half + 64, :]
            else:
                q = q_ref[2 * (tile - 8) + half, 128:192, :]
            q = jnp.concatenate([q, zeros] if half == 0 else [zeros, q], axis=0)
            s = mm(keys, q)
            buf[half] = s
            tops.append(jnp.max(s, axis=0, keepdims=True))
        return tops

    tops = scores(0)
    for tile in range(12):
        now = tops
        if tile < 11:
            tops = scores(tile + 1)
        vt = kv_ref[:, D + 128 * tile : D + 128 * tile + 128].T
        for half in range(2):
            head = 2 * tile + half
            p = jnp.exp(buffers[tile % 2][half] - now[half]).astype(BF16)
            acc = mm(jnp.concatenate([vt[64 * half : 64 * half + 64], ones], axis=0), p)
            total = acc[HD : HD + 1, :]
            o_ref[64 * head : 64 * head + 64, :] = (acc[0:HD, :] * (1.0 / total)).astype(BF16)
            lse_ref[head : head + 1, :] = now[half] + jnp.log(total)


def own(q, kv, tie):
    return pl.pallas_call(
        own_kernel,
        out_shape=(
            jax.ShapeDtypeStruct((D, ROWS), BF16),
            jax.ShapeDtypeStruct((HEADS, ROWS), F32),
        ),
        in_specs=[VMEM] * 2 + [ANY],
        out_specs=(VMEM,) * 2,
        scratch_shapes=[pltpu.VMEM((2, ROWS, ROWS), F32)] * 2,
        compiler_params=pltpu.CompilerParams(vmem_limit_bytes=12 * 2**20),
        cost_estimate=pl.CostEstimate(
            flops=16 * ROWS * ROWS * D, bytes_accessed=4 * 2**20, transcendentals=HEADS * ROWS * ROWS
        ),
        name="own_block",
    )(q, kv, tie)


CHUNK = 3
CHUNKS = 5
PAIR = 2
AHEAD = 2


def split3(x):
    hi = x.astype(BF16)
    rest = x - hi.astype(F32)
    mid = rest.astype(BF16)
    return hi, mid, (rest - mid.astype(F32)).astype(BF16)


def others_kernel(shift, chip_ref, q_ref, same_ref, pair_ref, tie_ref, o_ref, s_a, s_b):
    del tie_ref
    block = lax.rem(chip_ref[0] + shift + pl.program_id(0), CHIPS)
    zeros = jnp.zeros((HD, ROWS), BF16)
    qs = []
    for h in range(3):
        q = q_ref[0, 64 * h : 64 * h + 64, :]
        qs.append(
            (jnp.concatenate([q, zeros], axis=0), jnp.concatenate([zeros, q], axis=0))
        )
    places = [(same_ref, lax.rem(block + 1 + n, CHIPS)) for n in range(CHIPS - 1)]
    places += [(pair_ref, n) for n in range(CHIPS)]

    def key_parts(h, n):
        ref, b = places[n]
        if h < 2:
            return [(ref[b, 0:256, :], h)]
        packed = ref[b, 256:384, :]
        return [(packed, 0), (packed, 1)]

    def value_parts(h, ns):
        parts = []
        for n in ns:
            ref, b = places[n]
            for g in range(2):
                first = 384 + 192 * g + 64 * h
                parts.append(ref[b, first : first + 64, :])
        values = jnp.concatenate(parts, axis=1)
        return jnp.concatenate([values, jnp.ones((STATS, values.shape[1]), BF16)], axis=0)

    def emit(h, acc, top):
        total = acc[HD : HD + 1, :]
        o_ref[0, 64 * h : 64 * h + 64, :] = (acc[0:HD, :] * (1.0 / total)).astype(BF16)
        stats = split3(top + jnp.log(total))
        return list(stats)

    def write_stats(stats):
        stats = stats + [jnp.zeros((STATS - len(stats), ROWS), BF16)]
        o_ref[0, GROUP : GROUP + STATS, :] = jnp.concatenate(stats, axis=0)

    row = lax.broadcasted_iota(jnp.int32, (128, ROWS), 0)
    lanes = jnp.ones((ROWS, 128), BF16)
    first, tops, rhs = [], [], []
    for h in range(3):
        s = jnp.concatenate([mm(k, qs[h][i]) for k, i in key_parts(h, 0)], axis=0)
        top = jnp.max(s, axis=0, keepdims=True).astype(BF16).astype(F32)
        first.append(s)
        tops.append(top)
        minus = jnp.where(row == 0, -top, 0.0).astype(BF16)
        rhs.append([jnp.concatenate([q, minus], axis=0) for q in qs[h]])
    groups = [[0]] + [list(range(n, n + PAIR)) for n in range(1, 15, PAIR)]
    units = [(h, ns) for h in range(3) for ns in groups]

    def relative(h, ns):
        if ns == [0]:
            return first[h] - tops[h]
        outs = []
        for n in ns:
            for k, i in key_parts(h, n):
                outs.append(mm(jnp.concatenate([k, lanes[: k.shape[0]]], axis=1), rhs[h][i]))
        return jnp.concatenate(outs, axis=0)

    acc = [None] * 3
    waiting = [relative(*units[u]) for u in range(AHEAD)]
    for u, (h, ns) in enumerate(units):
        s = waiting.pop(0)
        if u + AHEAD < len(units):
            waiting.append(relative(*units[u + AHEAD]))
        out = mm(value_parts(h, ns), jnp.exp(s).astype(BF16))
        acc[h] = out if acc[h] is None else acc[h] + out
    stats = []
    good = None
    for h in range(3):
        stats += emit(h, acc[h], tops[h])
        total = acc[h][HD : HD + 1, :]
        size = jnp.sum(jnp.abs(acc[h]), axis=0, keepdims=True)
        ok = (total > 2.0**-20) & (total < 2.0**100) & (size < 2.0**126)
        good = ok if good is None else good & ok
    write_stats(stats)

    @pl.when(jnp.max(jnp.where(good, 0.0, 1.0)) > 0.5)
    def _():
        buffers = (s_a, s_b)
        units = [(h, c) for h in range(3) for c in range(CHUNKS)]

        def scores(u):
            h, c = units[u]
            buf = buffers[u % 2]
            top = None
            at = 0
            for n in range(c * CHUNK, (c + 1) * CHUNK):
                for k, i in key_parts(h, n):
                    s = mm(k, qs[h][i])
                    buf[at : at + s.shape[0], :] = s
                    at += s.shape[0]
                    m = jnp.max(s.reshape(-1, 8, ROWS), axis=0)
                    top = m if top is None else jnp.maximum(top, m)
            return jnp.max(top, axis=0, keepdims=True)

        tops = scores(0)
        top = acc = None
        stats = []
        for u, (h, c) in enumerate(units):
            new = tops if c == 0 else jnp.maximum(top, tops)
            if u + 1 < len(units):
                tops = scores(u + 1)
            p = jnp.exp(buffers[u % 2][...] - new).astype(BF16)
            out = mm(value_parts(h, range(c * CHUNK, (c + 1) * CHUNK)), p)
            acc = out if c == 0 else acc * jnp.exp(top - new) + out
            top = new
            if c == CHUNKS - 1:
                stats += emit(h, acc, top)
        write_stats(stats)


def others(chip, q, same, pair, tie, count, shift):
    place = lambda i, c: (lax.rem(c[0] + shift + i, CHIPS), 0, 0)
    out_place = place if count > 1 else lambda i, c: (0, 0, 0)
    return pl.pallas_call(
        functools.partial(others_kernel, shift),
        grid_spec=pltpu.PrefetchScalarGridSpec(
            num_scalar_prefetch=1,
            grid=(count,),
            in_specs=[pl.BlockSpec((1, GROUP, ROWS), place), VMEM, VMEM, ANY],
            out_specs=pl.BlockSpec((1, GROUP + STATS, ROWS), out_place),
            scratch_shapes=[pltpu.VMEM((CHUNK * ROWS, ROWS), F32)] * 2,
        ),
        out_shape=jax.ShapeDtypeStruct((CHIPS if count > 1 else 1, GROUP + STATS, ROWS), BF16),
        compiler_params=pltpu.CompilerParams(vmem_limit_bytes=16 * 2**20),
        cost_estimate=pl.CostEstimate(
            flops=count * 15 * 12 * ROWS * ROWS * HD * 4,
            bytes_accessed=4 * 2**20,
            transcendentals=count * 15 * 3 * ROWS * ROWS,
        ),
        name="other_blocks",
    )(chip, q, same, pair, tie)


def merge_kernel(
    chip_ref, o_ref, local_ref, own_ref, lse_ref, att
):
    part = [
        jnp.where(chip_ref[0] == j, local_ref[0], o_ref[j]).astype(F32) for j in range(CHIPS)
    ]
    for head in range(HEADS):
        if head < 16:
            chip, slot = head // 2, head % 2
        else:
            chip, slot = head - 16, 2
        parts = part[chip][GROUP : GROUP + STATS]
        there = parts[3 * slot : 3 * slot + 1] + parts[3 * slot + 1 : 3 * slot + 2]
        there = there + parts[3 * slot + 2 : 3 * slot + 3]
        here = lse_ref[head : head + 1, :]
        top = jnp.maximum(there, here)
        a = jnp.exp(there - top)
        b = jnp.exp(here - top)
        both = 1.0 / (a + b)
        rows = slice(64 * head, 64 * head + 64)
        merged = (
            part[chip][64 * slot : 64 * slot + 64] * (a * both)
            + own_ref[rows, :].astype(F32) * (b * both)
        )
        att[:, rows] = merged.astype(BF16).T


def merge(chip, o, local, own_o, lse):
    return pl.pallas_call(
        merge_kernel,
        out_shape=jax.ShapeDtypeStruct((ROWS, D), BF16),
        in_specs=[pl.BlockSpec(memory_space=pltpu.SMEM)] + [VMEM] * 4,
        out_specs=VMEM,
        compiler_params=pltpu.CompilerParams(vmem_limit_bytes=10 * 2**20),
        cost_estimate=pl.CostEstimate(
            flops=2**31, bytes_accessed=4 * 2**20, transcendentals=0
        ),
        name="merge",
    )(chip, o, local, own_o, lse)


def output_kernel(att_ref, gate_ref, mixed_ref, w_ref, out_ref):
    halves = 2
    width = D // halves
    for k in range(halves):
        cols = slice(k * width, (k + 1) * width)
        proj = mm(att_ref[...], w_ref[:, cols])
        out_ref[:, cols] = (mixed_ref[:, cols] + gate_ref[:, cols] * proj).astype(BF16)


def output(att, mixed, gate, w_out):
    return pl.pallas_call(
        output_kernel,
        out_shape=jax.ShapeDtypeStruct((ROWS, D), BF16),
        in_specs=[VMEM] * 4,
        out_specs=VMEM,
        compiler_params=pltpu.CompilerParams(vmem_limit_bytes=12 * 2**20),
        cost_estimate=pl.CostEstimate(
            flops=2 * ROWS * D * D, bytes_accessed=10 * 2**20, transcendentals=0
        ),
        name="output_projection",
    )(att, gate, mixed, w_out)


def per_device(
    latent, conv_weight, time_table, action_table, timestep, action, w_qkv, w_out, stale_kv
):
    count = lax.axis_size("patch")
    same_core = [list(range(c, count, 2)) for c in range(2)]

    def exchange(x):
        return lax.all_to_all(x, "patch", 0, 0, tiled=True, axis_index_groups=same_core)

    chip = (lax.axis_index("patch") // 2).astype(jnp.int32).reshape(1)
    patch = lax.axis_index("patch").astype(jnp.int32).reshape(1)
    top_row, last_row = latent[:GRID_W], latent[-GRID_W:]
    even = patch[0] % 2 == 0
    between = [(i, i + 1) for i in range(1, count - 1, 2)]
    packed, outer, inner = lax.optimization_barrier(
        (
            pack(stale_kv),
            jnp.where(even, top_row, last_row),
            jnp.where(even, last_row, top_row),
        )
    )
    outer = lax.ppermute(outer, "patch", between + [(b, a) for a, b in between])
    swap = [(i, i ^ 1) for i in range(count)]
    inner = lax.ppermute(inner, "patch", swap)
    same = exchange(packed)
    q, fresh_kv, mixed, gate = qkv(
        patch, timestep, action, latent, inner, outer, conv_weight, time_table, action_table, w_qkv
    )
    queries = exchange(q)
    same, _ = lax.optimization_barrier((same, gate))
    own_o, lse = own(q, fresh_kv, same)
    pair = lax.ppermute(same, "patch", swap)
    local = others(chip, q, same, pair, lse, 1, 0)
    remote = others(chip, queries, same, pair, local, CHIPS - 1, 1)
    attended = merge(chip, exchange(remote), local, own_o, lse)
    layer_out = output(attended, mixed, gate, w_out)
    return (layer_out, fresh_kv)


def solution(mesh):
    rows = P(("frame", "patch"), None)
    in_specs = (rows, P(), P(), P(), P("frame"), P("frame"), P(), P(), rows)
    return jax.shard_map(
        per_device, mesh=mesh, in_specs=in_specs, out_specs=(rows, rows), check_vma=False
    )
```
